256 devices in a mesh: ctx: 16 (over y_hi, z), tp: 4 (over y_lo, core), row: 4 (over x).
Axes of the slice: x: 4, y: 4 (y_hi: 2, y_lo: 2; y = y_hi * 2 + y_lo), z: 8, core: 2. Of those that a mesh axis runs over, the one named last changes fastest.
Arguments:
- queries: bfloat16 [512, 8, 8192], P('ctx', 'row', 'tp'), may hold values from -8 to 8
- new_keys: bfloat16 [512, 8, 1024], P('ctx', 'row', 'tp'), may hold values from -4 to 4
- new_values: bfloat16 [512, 8, 1024], P('ctx', 'row', 'tp'), may hold values from -6 to 6
- cache_keys: bfloat16 [8, 4096, 1024], P('row', 'ctx', 'tp'), may hold values from -4 to 4
- cache_values: bfloat16 [8, 4096, 1024], P('row', 'ctx', 'tp'), may hold values from -6 to 6
- out_proj: bfloat16 [8192, 8192], P('tp', ('ctx', 'row')), may hold values from -0.0625 to 0.0625
- skip_blocks: int32 [8], P('row'), may hold values from 1 to 4, 12 in all
- cache_len: int32 [8], P('row'), may hold values from 2048 to 4096, as said below
Outputs:
- projected: float32 [512, 8, 8192], P('tp', 'row', 'ctx')
The draws below stay inside these ranges and needn't reach their ends.
Inputs may be any that keep to these rules, and one draw needn't show every extreme that they name: `skip_blocks`: the counts sum to 12 and the largest is 4. `cache_len`: some row has exactly 4096.
All inputs are finite; a program needn't handle non-finite values. No bound on the sum of `skip_blocks` on one device may be relied on, other than what follows from the above.
Results may differ from the reference program's by a relative error of at most 0.008.
Values may be sent and summed in bfloat16 or wider, within the bound.
No kernel may reach another device: no remote copies, remote signals or barrier semaphores. Data moves between devices by JAX's collectives and lax.ppermute only.
A program may use at most 128 MiB of HBM per device.

```python
import math
import jax
import jax.numpy as jnp
import numpy as np
from jax import lax

D = 8192
KVH = 8
DH = 128
GROUP = 8
HQ = 64
BLOCK = 128
MOST_BLK = 4
QMAX = 512
ROWS = 8
CTX = 4096


def draw_queries(key, part):
    key = jax.random.fold_in(key, 11)
    values = jnp.clip(2.0 * jax.random.normal(key, (QMAX, ROWS, HQ * DH), jnp.float32), -8.0, 8.0)
    return values.astype(jnp.bfloat16)


def draw_cache_keys(key, part):
    key = jax.random.fold_in(key, 13)
    values = jnp.clip(jax.random.normal(key, (ROWS, CTX, KVH * DH), jnp.float32), -4.0, 4.0)
    return values.astype(jnp.bfloat16)


def draw_cache_len(key, part):
    key = jax.random.fold_in(key, 17)
    lowest = max(CTX // 2, QMAX + 2)
    lengths_drawn = jax.random.randint(key, (ROWS,), lowest, CTX + 1)
    chosen_row = jax.random.randint(jax.random.fold_in(key, 1), (), 0, ROWS)
    return jnp.where(jnp.arange(ROWS) == chosen_row, CTX, lengths_drawn).astype(jnp.int32)


def steps_of(rng, extent, shards, smallest, high):
    level, own = 1.0, jax.random.fold_in(rng, 6)
    for position, parts in shards:
        heights = jnp.exp(jax.random.uniform(jax.random.fold_in(own, position), (parts,), jnp.float32, smallest / len(shards), high / len(shards)))
        level = level * jnp.repeat(heights, extent[position] // parts).reshape([-1 if axis == position else 1 for axis in range(len(extent))])
    return level


def length_profile(amount, total, bound, skew):
    loads = [(1 << 20) // math.isqrt(rank ** skew) + 1 for rank in range(2, amount + 1)]
    surplus, counts = total - bound - (amount - 1), [1] * (amount - 1)
    while surplus > 0:
        free = [i for i in range(amount - 1) if counts[i] < bound]
        whole, budget = sum([loads[i] for i in free]), surplus
        for i in free:
            addition = min(bound - counts[i], max(1, budget * loads[i] // whole), surplus)
            counts[i] = counts[i] + addition
            surplus = surplus - addition
    return np.array([bound] + counts)


def ragged_sizes(stream_key, number_of, total, reach, slope):
    if number_of == 2:
        one = jax.random.randint(stream_key, (), max(1, total - reach), min(reach, total - 1) + 1)
        return jnp.stack([one, total - one])
    tallies = jnp.asarray(length_profile(number_of, total, reach, slope), jnp.int32)
    couples = (number_of - 1) // 2
    source_of, taker = tallies[1:1 + 2 * couples:2], tallies[2:2 + 2 * couples:2]
    slack = jnp.minimum(source_of - 1, reach - taker)
    shifted = jax.random.randint(jax.random.fold_in(stream_key, 1), (couples,), 0, 1 << 20) % (slack + 1)
    tallies = tallies.at[1:1 + 2 * couples:2].set(source_of - shifted).at[2:2 + 2 * couples:2].set(taker + shifted)
    return tallies[jax.random.permutation(jax.random.fold_in(stream_key, 2), number_of)]


def bell_draw(stream_key, shape, spread, bound, split=(), kind=jnp.bfloat16):
    array = spread * jax.random.normal(stream_key, shape, jnp.float32)
    if split:
        array = array * steps_of(stream_key, shape, split, -0.22, 0.18)
    return jnp.clip(array, -bound, bound).astype(kind)


def setup_inputs(seed: int = 0) -> dict:
    key_list = jax.random.split(jax.random.key(seed), 9)
    return {
        "queries": draw_queries(jax.random.fold_in(key_list[8], 71), 0),
        "new_keys": bell_draw(key_list[1], (QMAX, ROWS, KVH * DH), 1.0, 4.0, ((0, 16), (1, 4), (2, 4))),
        "new_values": bell_draw(key_list[2], (QMAX, ROWS, KVH * DH), 1.0, 6.0, ((0, 16), (1, 4), (2, 4))),
        "cache_keys": draw_cache_keys(jax.random.fold_in(key_list[8], 71), 0),
        "cache_values": bell_draw(key_list[4], (ROWS, CTX, KVH * DH), 1.0, 6.0, ((0, 4), (1, 16), (2, 4))),
        "out_proj": bell_draw(key_list[5], (HQ * DH, D), (HQ * DH) ** -0.5, 0.0625, ((0, 4), (1, 64))),
        "skip_blocks": ragged_sizes(key_list[6], ROWS, ROWS + ROWS // 2, MOST_BLK, 2).astype(jnp.int32),
        "cache_len": draw_cache_len(jax.random.fold_in(key_list[8], 71), 0),
    }


masked_score = -1.0e30


def reference(queries, new_keys, new_values, cache_keys, cache_values, out_proj, skip_blocks, cache_len):
    token_count = skip_blocks * BLOCK
    first_slot = cache_len - token_count
    score_scale = DH ** -0.5
    positions = jnp.arange(CTX, dtype=jnp.int32)
    tokens = jnp.arange(QMAX, dtype=jnp.int32)
    causal = tokens[None, :] <= tokens[:, None]
    query_heads = jnp.transpose(queries.reshape(QMAX, ROWS, KVH, GROUP, DH), (1, 2, 3, 0, 4))
    new_key_heads = jnp.transpose(new_keys.reshape(QMAX, ROWS, KVH, DH), (1, 2, 0, 3))
    new_value_heads = jnp.transpose(new_values.reshape(QMAX, ROWS, KVH, DH), (1, 2, 0, 3))
    cache_key_heads = jnp.transpose(cache_keys.reshape(ROWS, CTX, KVH, DH), (0, 2, 1, 3))
    cache_value_heads = jnp.transpose(cache_values.reshape(ROWS, CTX, KVH, DH), (0, 2, 1, 3))

    def per_row(row_items):
        row_queries, row_new_keys, row_new_values, row_cache_keys, row_cache_values, row_first, row_count = row_items
        cached = positions < row_first
        allowed = jnp.concatenate([jnp.broadcast_to(cached[None, :], (QMAX, CTX)), causal], axis=1)
        valid = tokens < row_count

        def per_group(group_items):
            group_queries, group_new_keys, group_new_values, group_cache_keys, group_cache_values = group_items
            key_rows = jnp.concatenate([group_cache_keys, group_new_keys], axis=0).astype(jnp.float32)
            value_rows = jnp.concatenate([group_cache_values, group_new_values], axis=0)

            def per_head(head_queries):
                scores = jnp.dot(head_queries.astype(jnp.float32), key_rows.T, precision=lax.Precision.HIGHEST) * score_scale
                scores = jnp.where(allowed, scores, masked_score)
                highest = jnp.max(scores, axis=1, keepdims=True)
                weights = jnp.where(allowed, jnp.exp(scores - highest), 0.0)
                totals = jnp.sum(weights, axis=1, keepdims=True)
                low_weights = weights.astype(jnp.bfloat16)
                mixed = jnp.dot(low_weights, value_rows, preferred_element_type=jnp.float32) / totals
                return jnp.where(valid[:, None], mixed, 0.0)

            return lax.map(per_head, group_queries)

        return lax.map(per_group, (row_queries, row_new_keys, row_new_values, row_cache_keys, row_cache_values))

    heads_out = lax.map(per_row, (query_heads, new_key_heads, new_value_heads, cache_key_heads, cache_value_heads, first_slot, token_count))
    attended = jnp.transpose(heads_out, (3, 0, 1, 2, 4)).reshape(QMAX, ROWS, HQ * DH).astype(jnp.bfloat16)
    flat_rows = attended.reshape(QMAX * ROWS, HQ * DH)
    projected = jnp.dot(flat_rows, out_proj, preferred_element_type=jnp.float32)
    return projected.reshape(QMAX, ROWS, D)
```

```python
import jax
import jax.numpy as jnp
from jax import lax
from jax.experimental import pallas as pl
from jax.experimental.pallas import tpu as pltpu
from jax.sharding import Mesh, PartitionSpec as P

DH = 128
BLOCK = 128
SLOTS = 256
PART = 1152
masked_score = -1e30
exp2_scale = DH ** -0.5 * 1.4426950408889634

VMEM = pl.BlockSpec(memory_space=pltpu.VMEM)
SMEM = pl.BlockSpec(memory_space=pltpu.SMEM)
PARAMS = pltpu.CompilerParams(vmem_limit_bytes=48 * 1024 * 1024)


def columns_of(index):
    return pl.ds(pl.multiple_of(index * DH, DH), DH)


def pack_kernel(place, cache_keys, cache_values, new_keys, new_values, own, other):
    high = place[0]
    for target, head in ((own, high), (other, 1 - high)):
        columns = columns_of(head)
        for row in range(2):
            target[SLOTS * row : SLOTS * (row + 1)] = cache_keys[row, :, columns]
            target[512 + SLOTS * row : 512 + SLOTS * (row + 1)] = cache_values[row, :, columns]
        target[1024:1088] = new_keys[:, columns]
        target[1088:1152] = new_values[:, columns]


def pack(place, cache_keys, cache_values, new_keys, new_values):
    shape = jax.ShapeDtypeStruct((PART, DH), jnp.bfloat16)
    return pl.pallas_call(
        pack_kernel,
        out_shape=(shape, shape),
        in_specs=[SMEM] + [VMEM] * 4,
        out_specs=(VMEM, VMEM),
        compiler_params=PARAMS,
    )(place, cache_keys, cache_values, new_keys, new_values)


def attend_kernel(offsets, place, queries, *refs):
    parts = refs[: len(offsets)]
    out, flat_keys, flat_values, sorted_queries, new_keys, new_values, scores = refs[len(offsets) :]
    high, ring = place[0], place[1]
    sources = []
    for distance, is_own in offsets:
        source_ring = lax.rem(ring + distance, 8)
        sources.append((high if is_own else 1 - high) * 8 + source_ring)
    for part, source in zip(parts, sources):
        where = pl.ds(pl.multiple_of(source * 64, 64), 64)
        flat_keys[where] = part[1024:1088]
        flat_values[where] = part[1088:1152]
    target = lax.broadcasted_iota(jnp.int32, (256, 256), 0)
    origin = lax.broadcasted_iota(jnp.int32, (256, 256), 1)
    wanted = jnp.where(target < 128, 2 * target, 2 * target - 255)
    permute = (origin == wanted).astype(jnp.float32).astype(jnp.bfloat16)
    for block in range(4):
        for flat, split in ((queries, sorted_queries), (flat_keys, new_keys), (flat_values, new_values)):
            moved = jnp.dot(
                permute, flat[256 * block : 256 * (block + 1)], preferred_element_type=jnp.float32
            ).astype(jnp.bfloat16)
            split[0, 128 * block : 128 * (block + 1)] = moved[:128]
            split[1, 128 * block : 128 * (block + 1)] = moved[128:]
    out[...] = jnp.zeros_like(out)
    larger = (place[3] > place[2]).astype(jnp.int32)

    def score(query, key):
        return lax.dot_general(
            query, key, (((1,), (1,)), ((), ())), preferred_element_type=jnp.float32
        )

    for row in range(2):
        count, first = place[2 + row], place[4 + row]

        def unit(block, carry):
            query = sorted_queries[row, pl.ds(pl.multiple_of(block * 128, 128), 128), :]
            lane = lax.broadcasted_iota(jnp.int32, (128, 256), 1)
            peak = jnp.full((128, 128), masked_score, jnp.float32)
            for index, (part, source) in enumerate(zip(parts, sources)):
                found = score(query, part[SLOTS * row : SLOTS * (row + 1)])
                found = jnp.where(lane < first - source * SLOTS, found, masked_score)
                scores[:, SLOTS * index : SLOTS * (index + 1)] = found
                peak = jnp.maximum(peak, jnp.maximum(found[:, :128], found[:, 128:]))
            base = SLOTS * len(parts)
            token = lax.broadcasted_iota(jnp.int32, (128, 128), 0) + block * 128
            fresh = lax.broadcasted_iota(jnp.int32, (128, 128), 1)
            for index in range(4):
                found = score(query, new_keys[row, 128 * index : 128 * (index + 1)])
                found = jnp.where(fresh + 128 * index <= token, found, masked_score)
                scores[:, base + 128 * index : base + 128 * (index + 1)] = found
                peak = jnp.maximum(peak, found)
            top = jnp.max(peak, axis=1, keepdims=True)
            total = jnp.zeros((128, 128), jnp.float32)
            mixed = jnp.zeros((128, DH), jnp.float32)
            for index, part in enumerate(parts):
                weight = jnp.exp2(
                    (scores[:, SLOTS * index : SLOTS * (index + 1)] - top) * exp2_scale
                )
                total = total + (weight[:, :128] + weight[:, 128:])
                mixed = mixed + jnp.dot(
                    weight.astype(jnp.bfloat16),
                    part[512 + SLOTS * row : 512 + SLOTS * (row + 1)],
                    preferred_element_type=jnp.float32,
                )
            for index in range(4):
                weight = jnp.exp2(
                    (scores[:, base + 128 * index : base + 128 * (index + 1)] - top) * exp2_scale
                )
                total = total + weight
                mixed = mixed + jnp.dot(
                    weight.astype(jnp.bfloat16),
                    new_values[row, 128 * index : 128 * (index + 1)],
                    preferred_element_type=jnp.float32,
                )
            result = (mixed / jnp.sum(total, axis=1, keepdims=True)).astype(jnp.bfloat16)
            slot = jnp.where(block < 2, block * 3 + row, block * 3 - 4)
            out[pl.ds(pl.multiple_of(slot * 128, 128), 128), :] = result
            return carry

        lax.fori_loop(0, jnp.where(larger == row, count, jnp.minimum(count, 2)), unit, 0)


def attend(place, queries, parts, offsets):
    keys = SLOTS * len(parts) + 512
    return pl.pallas_call(
        lambda *refs: attend_kernel(offsets, *refs),
        out_shape=jax.ShapeDtypeStruct((768, DH), jnp.bfloat16),
        in_specs=[SMEM] + [VMEM] * (1 + len(parts)),
        out_specs=VMEM,
        scratch_shapes=[
            pltpu.VMEM((1024, DH), jnp.bfloat16),
            pltpu.VMEM((1024, DH), jnp.bfloat16),
            pltpu.VMEM((2, 512, DH), jnp.bfloat16),
            pltpu.VMEM((2, 512, DH), jnp.bfloat16),
            pltpu.VMEM((2, 512, DH), jnp.bfloat16),
            pltpu.VMEM((128, keys), jnp.float32),
        ],
        compiler_params=PARAMS,
    )(place, queries, *parts)


def project_kernel(place, *refs):
    attended = refs[:8]
    weights, kept, sent, gathered = refs[8:]
    ring, core = place[1], place[6]
    for distance in range(8):
        gathered[:, columns_of(lax.rem(ring + distance, 8))] = attended[distance][...]
    for target, owner in ((sent, 1 - core), (kept, core)):
        rows = gathered[pl.ds(pl.multiple_of(owner * 384, 128), 384), :]
        for side in range(2):
            for pair in range(2):
                block = jnp.concatenate(
                    [weights[2 * pair, side], weights[2 * pair + 1, side]], axis=1
                )
                target[side, :, 256 * pair : 256 * (pair + 1)] = jnp.dot(
                    rows, block, preferred_element_type=jnp.float32
                ).astype(target.dtype)


def project(place, attended, weights):
    return pl.pallas_call(
        project_kernel,
        out_shape=(
            jax.ShapeDtypeStruct((2, 384, 512), jnp.float32),
            jax.ShapeDtypeStruct((2, 384, 512), jnp.bfloat16),
        ),
        in_specs=[SMEM] + [VMEM] * 9,
        out_specs=(VMEM, VMEM),
        scratch_shapes=[pltpu.VMEM((768, 1024), jnp.bfloat16)],
        compiler_params=PARAMS,
    )(place, *attended, weights)


def add_kernel(place, kept, arrived, out):
    high = place[0]
    for side in range(2):
        owner = high if side == 0 else 1 - high
        total = kept[side] + arrived[side].astype(jnp.float32)
        out[owner * 2] = total[:256].astype(jnp.bfloat16)
        out[owner * 2 + 1, :128] = total[256:].astype(jnp.bfloat16)
        out[owner * 2 + 1, 128:] = jnp.zeros((128, 512), jnp.bfloat16)


def add_cores(place, kept, arrived):
    return pl.pallas_call(
        add_kernel,
        out_shape=jax.ShapeDtypeStruct((4, 256, 512), jnp.bfloat16),
        in_specs=[SMEM, VMEM, VMEM],
        out_specs=VMEM,
        compiler_params=PARAMS,
    )(place, kept, arrived)


def final_kernel(place, arrived, out):
    low = place[7]
    total = arrived[0].astype(jnp.float32)
    for source in range(1, 4):
        total = total + arrived[source].astype(jnp.float32)
    larger = place[3] > place[2]
    first, second = total[:128], total[128:]
    zero = jnp.zeros_like(first)
    first_row = jnp.where(low == 0, first, jnp.where(larger, zero, first))
    second_row = jnp.where(low == 0, second, jnp.where(larger, first, zero))
    out[:, 0, :] = first_row
    out[:, 1, :] = second_row


def finish(place, arrived):
    return pl.pallas_call(
        final_kernel,
        out_shape=jax.ShapeDtypeStruct((128, 2, 512), jnp.float32),
        in_specs=[SMEM, VMEM],
        out_specs=VMEM,
        compiler_params=PARAMS,
    )(place, arrived)


UP = [(index, (index + 1) % 8) for index in range(8)]
DOWN = [(index, (index + 7) % 8) for index in range(8)]
SWAP = [(0, 1), (1, 0)]


def on_device(
    queries, new_keys, new_values, cache_keys, cache_values, out_proj, skip_blocks, cache_len
):
    high, ring = lax.axis_index("yh"), lax.axis_index("z")
    low, core = lax.axis_index("yl"), lax.axis_index("co")
    first_slot = cache_len - skip_blocks * BLOCK
    place = jnp.concatenate(
        [
            jnp.stack([high, ring]).astype(jnp.int32),
            skip_blocks,
            first_slot,
            jnp.stack([core, low]).astype(jnp.int32),
        ]
    )
    own, other = pack(
        place,
        cache_keys,
        cache_values,
        new_keys.reshape(64, 256),
        new_values.reshape(64, 256),
    )
    partner = lax.ppermute(other, "yh", SWAP)
    split_queries = jnp.transpose(queries.reshape(32, 2, 16, DH), (2, 0, 1, 3)).reshape(16, 64, DH)
    got_queries = lax.all_to_all(
        split_queries, ("yh", "z"), split_axis=0, concat_axis=0, tiled=True
    ).reshape(1024, DH)

    half = lax.dynamic_slice_in_dim(out_proj, (1 - high) * 1024, 1024, 0)
    kept_half = lax.dynamic_slice_in_dim(out_proj, high * 1024, 1024, 0)
    got_half = lax.ppermute(half, "yh", SWAP)
    weights = lax.all_gather(jnp.stack([kept_half, got_half]), "row", axis=0, tiled=False)

    parts, offsets = [own, partner], [(0, True), (0, False)]
    own_up, own_down, partner_up, partner_down = own, own, partner, partner
    for step in range(1, 5):
        own_down = lax.ppermute(own_down, "z", DOWN)
        parts.append(own_down)
        offsets.append((step, True))
        partner_up = lax.ppermute(partner_up, "z", UP)
        parts.append(partner_up)
        offsets.append((8 - step, False))
        if step < 4:
            own_up = lax.ppermute(own_up, "z", UP)
            parts.append(own_up)
            offsets.append((8 - step, True))
            partner_down = lax.ppermute(partner_down, "z", DOWN)
            parts.append(partner_down)
            offsets.append((step, False))
    attended = attend(place, got_queries, parts, offsets)

    gathered = [attended] + [None] * 7
    going_up, going_down = attended, attended
    for step in range(1, 5):
        going_down = lax.ppermute(going_down, "z", DOWN)
        gathered[step] = going_down
        if step < 4:
            going_up = lax.ppermute(going_up, "z", UP)
            gathered[8 - step] = going_up
    kept, sent = project(place, gathered, weights)
    arrived = lax.ppermute(sent, "co", SWAP)
    merged = add_cores(place, kept, arrived)
    shares = lax.all_to_all(merged, ("yh", "yl"), split_axis=0, concat_axis=0, tiled=True)
    return finish(place, shares)


def solution(mesh):
    split = Mesh(mesh.devices.reshape(2, 8, 2, 2, 4), ("yh", "z", "yl", "co", "row"))
    ctx, tp = ("yh", "z"), ("yl", "co")
    placed = (
        P(ctx, "row", tp),
        P(ctx, "row", tp),
        P(ctx, "row", tp),
        P("row", ctx, tp),
        P("row", ctx, tp),
        P(tp, ("yh", "z", "row")),
        P("row"),
        P("row"),
    )
    return jax.shard_map(
        on_device, mesh=split, in_specs=placed, out_specs=P(tp, "row", ctx), check_vma=False
    )
```

```python
import jax
import jax.numpy as jnp
from jax import lax
from jax.experimental import pallas as pl
from jax.experimental.pallas import tpu as pltpu
from jax.sharding import Mesh, PartitionSpec as P

DH = 128
BLOCK = 128
SLOTS = 256
PART = 1152
masked_score = -1e30
exp2_scale = DH ** -0.5 * 1.4426950408889634

VMEM = pl.BlockSpec(memory_space=pltpu.VMEM)
SMEM = pl.BlockSpec(memory_space=pltpu.SMEM)
PARAMS = pltpu.CompilerParams(vmem_limit_bytes=48 * 1024 * 1024)


def columns_of(index):
    return pl.ds(pl.multiple_of(index * DH, DH), DH)


def location():
    return {name: lax.axis_index(name) for name in ("yh", "z", "yl", "co")}


def bring(outside, held, arrived):
    copies = [
        pltpu.make_async_copy(source, target, arrived.at[index])
        for index, (source, target) in enumerate(zip(outside, held))
    ]
    for copy in copies:
        copy.start()
    for copy in copies:
        copy.wait()


def pack_kernel(*refs):
    outside, (own, other, split_queries), held, arrived = refs[:5], refs[5:8], refs[8:13], refs[13]
    bring(outside, held, arrived)
    cache_keys, cache_values, new_keys, new_values, queries = held
    high = location()["yh"]
    for target, head in ((own, high), (other, 1 - high)):
        columns = columns_of(head)
        for row in range(2):
            target[SLOTS * row : SLOTS * (row + 1)] = cache_keys[row, :, columns]
            target[512 + SLOTS * row : 512 + SLOTS * (row + 1)] = cache_values[row, :, columns]
        target[1024:1088] = new_keys[:, :, columns].reshape(64, DH)
        target[1088:1152] = new_values[:, :, columns].reshape(64, DH)
    for head in range(16):
        piece = queries[:, :, DH * head : DH * (head + 1)].reshape(64, DH)
        split_queries[head, 0] = piece
        split_queries[head // 8 * 8 + (head + 4) % 8, 1] = piece


def with_copies(kernel, arrays, out_shape, **options):
    return pl.pallas_call(
        kernel,
        out_shape=out_shape,
        in_specs=[pl.BlockSpec(memory_space=pl.ANY)] * len(arrays),
        out_specs=jax.tree.map(lambda _: VMEM, out_shape),
        scratch_shapes=[pltpu.VMEM(array.shape, array.dtype) for array in arrays]
        + [pltpu.SemaphoreType.DMA((len(arrays),))],
        compiler_params=pltpu.CompilerParams(vmem_limit_bytes=60 * 1024 * 1024),
        **options,
    )(*arrays)


def pack(*arrays):
    shape = jax.ShapeDtypeStruct((PART, DH), jnp.bfloat16)
    return with_copies(
        pack_kernel, arrays, (shape, shape, jax.ShapeDtypeStruct((16, 2, 64, DH), jnp.bfloat16))
    )


def score(query, key):
    return lax.dot_general(
        query, key, (((1,), (1,)), ((), ())), preferred_element_type=jnp.float32
    )


def sort_rows(flat):
    target = lax.broadcasted_iota(jnp.int32, (256, 256), 0)
    origin = lax.broadcasted_iota(jnp.int32, (256, 256), 1)
    wanted = jnp.where(target < 128, 2 * target, 2 * target - 255)
    permute = (origin == wanted).astype(jnp.float32).astype(jnp.bfloat16)
    moved = jnp.dot(permute, flat, preferred_element_type=jnp.float32).astype(jnp.bfloat16)
    return moved[:128], moved[128:]


def attend_kernel(offsets, head, skip_blocks, cache_len, queries, *refs):
    high, ring = location()["yh"], location()["z"]
    sources = [
        (high if is_own else 1 - high) * 8 + lax.rem(ring + distance, 8)
        for distance, is_own in offsets
    ]
    parts, refs = refs[: len(offsets)], refs[len(offsets) :]
    if head == 0:
        mine, own_level, sorted_queries, new_keys, new_values, scores = refs
    else:
        message, sorted_queries, new_keys, new_values, scores, statistics = refs
        statistics[...] = jnp.zeros_like(statistics)
    for group in range(4):
        flat = queries[4 * group : 4 * group + 4, head].reshape(256, DH)
        first_row, second_row = sort_rows(flat)
        sorted_queries[0, 128 * group : 128 * (group + 1)] = first_row
        sorted_queries[1, 128 * group : 128 * (group + 1)] = second_row
    for group in range(2):
        for start, sorted_rows in ((1024, new_keys), (1088, new_values)):
            flat = jnp.concatenate(
                [part[start : start + 64] for part in parts[4 * group : 4 * group + 4]], axis=0
            )
            first_row, second_row = sort_rows(flat)
            sorted_rows[0, 128 * group : 128 * (group + 1)] = first_row
            sorted_rows[1, 128 * group : 128 * (group + 1)] = second_row
    lane = lax.broadcasted_iota(jnp.int32, (1, 256), 1)
    new_token = lane % 32
    for index, source in enumerate(sources):
        new_token = new_token + jnp.where(lane // 32 == index, source * 32, 0)
    larger = (skip_blocks[1] > skip_blocks[0]).astype(jnp.int32)
    most = jnp.maximum(skip_blocks[0], skip_blocks[1])
    fewer = jnp.minimum(skip_blocks[0], skip_blocks[1])
    diagonal = lax.broadcasted_iota(jnp.int32, (128, 128), 0) == lax.broadcasted_iota(
        jnp.int32, (128, 128), 1
    )

    for index in range(3):
        row = 1 - larger if index == 1 else larger
        count = fewer if index == 1 else most
        block = 2 if index == 2 else 0
        slot = 2 if index == 2 else row
        first = jnp.where(row == 0, cache_len[0], cache_len[1]) - count * BLOCK
        key_rows = pl.ds(pl.multiple_of(row * SLOTS, SLOTS), SLOTS)
        value_rows = pl.ds(pl.multiple_of(row * SLOTS + 512, SLOTS), SLOTS)
        query = sorted_queries[row, pl.ds(block * 128, 256), :]
        peak = jnp.full((256, 128), masked_score, jnp.float32)
        spans = []
        for place_in, (part, source) in enumerate(zip(parts, sources)):
            bias = jnp.where(lane < first - source * SLOTS, 0.0, masked_score)
            found = score(query, part[key_rows]) + bias
            span = slice(SLOTS * place_in, SLOTS * (place_in + 1))
            scores[index, :, span] = found
            spans.append((span, lambda part=part: part[value_rows]))
            peak = jnp.maximum(peak, jnp.maximum(found[:, :128], found[:, 128:]))
        token = lax.broadcasted_iota(jnp.int32, (256, 1), 0) + block * 128
        found = score(query, new_keys[row])
        found = jnp.where(new_token <= token, found, masked_score)
        span = slice(SLOTS * len(parts), SLOTS * (len(parts) + 1))
        scores[index, :, span] = found
        spans.append((span, lambda: new_values[row]))
        peak = jnp.maximum(peak, jnp.maximum(found[:, :128], found[:, 128:]))
        top = jnp.broadcast_to(jnp.max(peak, axis=1, keepdims=True), (256, 128))
        total = jnp.zeros((256, 128), jnp.float32)
        mixed = jnp.zeros((256, DH), jnp.float32)
        wide = jnp.concatenate([top, top], axis=1)
        for span, values in spans:
            weight = jnp.exp2((scores[index, :, span] - wide) * exp2_scale)
            total = total + (weight[:, :128] + weight[:, 128:])
            mixed = mixed + jnp.dot(
                weight.astype(jnp.bfloat16), values(), preferred_element_type=jnp.float32
            )
        whole = jnp.broadcast_to(jnp.sum(total, axis=1, keepdims=True), (256, 128))
        result = mixed / whole
        level = top * exp2_scale + jnp.log2(whole)
        result = jnp.concatenate(
            [
                jnp.where(count > block, result[:128], 0.0),
                jnp.where(count > block + 1, result[128:], 0.0),
            ],
            axis=0,
        )
        for half in range(2):
            here = slot + 3 * half
            rows = pl.ds(here * 128, 128)
            if index < 2:
                rows = pl.ds(pl.multiple_of(here * 128, 128), 128)
            piece = result[128 * half : 128 * (half + 1)]
            piece_level = level[128 * half : 128 * (half + 1)]
            if head == 0:
                mine[rows, :] = piece
                own_level[rows, :] = piece_level
            else:
                message[rows, :] = piece.astype(jnp.bfloat16)
                flat = jnp.sum(jnp.where(diagonal, piece_level, 0.0), axis=0, keepdims=True)
                for term in range(3):
                    rounded = flat.astype(jnp.bfloat16).astype(jnp.float32)
                    statistics[pl.ds(term * 8 + here, 1), :] = rounded
                    flat = flat - rounded
    if head == 1:
        message[768:800] = statistics[...].astype(jnp.bfloat16)


def attend(counts, queries, parts, offsets, head):
    scratch = [
        pltpu.VMEM((2, 512, DH), jnp.bfloat16),
        pltpu.VMEM((2, 256, DH), jnp.bfloat16),
        pltpu.VMEM((2, 256, DH), jnp.bfloat16),
        pltpu.VMEM((3, 256, SLOTS * (len(parts) + 1)), jnp.float32),
    ]
    if head == 0:
        out_shape = (jax.ShapeDtypeStruct((768, DH), jnp.float32),) * 2
        out_specs = (VMEM,) * 2
    else:
        out_shape = jax.ShapeDtypeStruct((800, DH), jnp.bfloat16)
        out_specs = VMEM
        scratch.append(pltpu.VMEM((32, DH), jnp.float32))
    return pl.pallas_call(
        lambda *refs: attend_kernel(offsets, head, *refs),
        out_shape=out_shape,
        in_specs=[SMEM] * 2 + [VMEM] * (1 + len(parts)),
        out_specs=out_specs,
        scratch_shapes=scratch,
        compiler_params=PARAMS,
        cost_estimate=pl.CostEstimate(
            flops=5 * 10**9, bytes_accessed=6 * 2**20, transcendentals=2 * 10**6
        ),
    )(*counts, queries, *parts)


def merge_kernel(mine, own_level, message, out):
    diagonal = lax.broadcasted_iota(jnp.int32, (128, 128), 0) == lax.broadcasted_iota(
        jnp.int32, (128, 128), 1
    )
    statistics = message[768:800].astype(jnp.float32)
    for slot in range(6):
        rows = slice(128 * slot, 128 * (slot + 1))
        flat = (
            statistics[slot : slot + 1]
            + statistics[8 + slot : 9 + slot]
            + statistics[16 + slot : 17 + slot]
        )
        level = jnp.sum(jnp.where(diagonal, flat, 0.0), axis=1, keepdims=True)
        top = jnp.maximum(own_level[rows], level)
        own_weight = jnp.exp2(own_level[rows] - top)
        other_weight = jnp.exp2(level - top)
        mixed = own_weight * mine[rows] + other_weight * message[rows].astype(jnp.float32)
        out[rows] = (mixed / (own_weight + other_weight)).astype(jnp.bfloat16)


def merge(mine, own_level, message):
    return pl.pallas_call(
        merge_kernel,
        out_shape=jax.ShapeDtypeStruct((768, DH), jnp.bfloat16),
        in_specs=[VMEM] * 3,
        out_specs=VMEM,
        compiler_params=PARAMS,
    )(mine, own_level, message)


def project_kernel(*refs):
    attended = refs[:9]
    kept_half, got_half, kept, sent, gathered = refs[9:]
    ring, core = location()["z"], location()["co"]
    for distance in range(8):
        columns = columns_of(lax.rem(ring + distance, 8))
        if distance == 4:
            gathered[:384, columns] = attended[4][...]
            gathered[384:, columns] = attended[8][...]
        else:
            gathered[:, columns] = attended[distance][...]
    for target, owner in ((sent, 1 - core), (kept, core)):
        rows = gathered[pl.ds(pl.multiple_of(owner * 384, 128), 384), :]
        for side, weights in enumerate((kept_half, got_half)):
            for pair in range(2):
                block = jnp.concatenate([weights[2 * pair], weights[2 * pair + 1]], axis=1)
                target[side, :, 256 * pair : 256 * (pair + 1)] = jnp.dot(
                    rows, block, preferred_element_type=jnp.float32
                ).astype(target.dtype)


def project(attended, kept_half, got_half):
    return pl.pallas_call(
        project_kernel,
        out_shape=(
            jax.ShapeDtypeStruct((2, 384, 512), jnp.float32),
            jax.ShapeDtypeStruct((2, 384, 512), jnp.bfloat16),
        ),
        in_specs=[VMEM] * 11,
        out_specs=(VMEM, VMEM),
        scratch_shapes=[pltpu.VMEM((768, 1024), jnp.bfloat16)],
        compiler_params=PARAMS,
    )(*attended, kept_half, got_half)


def add_kernel(kept, arrived, mine, near, far, cross):
    low = location()["yl"]
    for side, targets in ((0, (mine, near)), (1, (far, cross))):
        total = kept[side] + arrived[side].astype(jnp.float32)
        pair = total[:256]
        single = jnp.concatenate([total[256:], jnp.zeros((128, 512), jnp.float32)], axis=0)
        targets[0][...] = jnp.where(low == 0, pair, single).astype(targets[0].dtype)
        targets[1][...] = jnp.where(low == 0, single, pair).astype(targets[1].dtype)


def add_cores(kept, arrived):
    shape = jax.ShapeDtypeStruct((256, 512), jnp.bfloat16)
    return pl.pallas_call(
        add_kernel,
        out_shape=(jax.ShapeDtypeStruct((256, 512), jnp.float32), shape, shape, shape),
        in_specs=[VMEM, VMEM],
        out_specs=(VMEM,) * 4,
        compiler_params=PARAMS,
    )(kept, arrived)


def final_kernel(skip_blocks, mine, near, far, cross, out):
    low = location()["yl"]
    total = mine[...]
    for share in (near, far, cross):
        total = total + share[...].astype(jnp.float32)
    larger = skip_blocks[1] > skip_blocks[0]
    first, second = total[:128], total[128:]
    zero = jnp.zeros_like(first)
    first_row = jnp.where(low == 0, first, jnp.where(larger, zero, first))
    second_row = jnp.where(low == 0, second, jnp.where(larger, first, zero))
    out[:, 0, :] = first_row
    out[:, 1, :] = second_row


def finish(skip_blocks, *shares):
    return pl.pallas_call(
        final_kernel,
        out_shape=jax.ShapeDtypeStruct((128, 2, 512), jnp.float32),
        in_specs=[SMEM] + [VMEM] * 4,
        out_specs=VMEM,
        compiler_params=PARAMS,
    )(skip_blocks, *shares)


SWAP = [(0, 1), (1, 0)]


def ring_send(array, hops):
    return lax.ppermute(array, "z", [(index, (index + hops) % 8) for index in range(8)])


def on_device(
    queries, new_keys, new_values, cache_keys, cache_values, out_proj, skip_blocks, cache_len
):
    high = lax.axis_index("yh")
    counts = (skip_blocks, cache_len)
    own, other, split_queries = pack(cache_keys, cache_values, new_keys, new_values, queries)
    partner = lax.ppermute(other, "yh", SWAP)
    own_up, own_down = ring_send(own, 1), ring_send(own, -1)
    got_queries = lax.all_to_all(
        split_queries, ("yh", "z"), split_axis=0, concat_axis=0, tiled=True
    )
    partner_up, partner_down = ring_send(partner, 1), ring_send(partner, -1)
    own_down_two = ring_send(own_down, -1)
    tied_up, own_up = lax.optimization_barrier((partner_up, own_up))
    partner_up_two = ring_send(tied_up, 1)
    parts = [own, partner, own_up, own_down, own_down_two, partner_up, partner_down, partner_up_two]
    offsets = [
        (0, True), (0, False), (7, True), (1, True), (2, True), (7, False), (1, False), (6, False)
    ]
    out_proj, own = lax.optimization_barrier((out_proj, own))
    weights = lax.all_gather(out_proj, "row", axis=0, tiled=False)
    weights, _ = lax.optimization_barrier((weights, tied_up))
    sent_half = lax.dynamic_slice_in_dim(weights, (1 - high) * 1024, 1024, 1)
    kept_half = lax.dynamic_slice_in_dim(weights, high * 1024, 1024, 1)
    got_half = lax.ppermute(sent_half, "yh", SWAP)
    message = attend(counts, got_queries, parts, offsets, 1)
    mine, own_level = attend(counts, got_queries, parts, offsets, 0)
    attended = merge(mine, own_level, ring_send(message, 4))

    from_below, from_above = ring_send(attended, 1), ring_send(attended, -1)
    two_below, two_above = ring_send(attended, 2), ring_send(attended, -2)
    gathered = [
        attended,
        from_above,
        two_above,
        ring_send(two_above, -1),
        ring_send(two_below[:384], 2),
        ring_send(two_below, 1),
        two_below,
        from_below,
        ring_send(two_above[384:], -2),
    ]
    kept, sent = project(gathered, kept_half, got_half)
    arrived = lax.ppermute(sent, "co", SWAP)
    mine, near, far, cross = add_cores(kept, arrived)
    far = lax.ppermute(far, "yh", SWAP)
    cross = lax.ppermute(cross, ("yh", "yl"), [(0, 3), (1, 2), (2, 1), (3, 0)])
    near = lax.ppermute(near, "yl", SWAP)
    return finish(skip_blocks, mine, near, far, cross)


def solution(mesh):
    split = Mesh(mesh.devices.reshape(2, 8, 2, 2, 4), ("yh", "z", "yl", "co", "row"))
    ctx, tp = ("yh", "z"), ("yl", "co")
    placed = (
        P(ctx, "row", tp),
        P(ctx, "row", tp),
        P(ctx, "row", tp),
        P("row", ctx, tp),
        P("row", ctx, tp),
        P(tp, ("yh", "z", "row")),
        P("row"),
        P("row"),
    )
    return jax.shard_map(
        on_device, mesh=split, in_specs=placed, out_specs=P(tp, "row", ctx), check_vma=False
    )
```

```python
import jax
import jax.numpy as jnp
from jax import lax
from jax.experimental import pallas as pl
from jax.experimental.pallas import tpu as pltpu
from jax.sharding import Mesh, PartitionSpec as P

DH = 128
BLOCK = 128
SLOTS = 256
PART = 1152
masked_score = -1e30
exp2_scale = DH ** -0.5 * 1.4426950408889634

VMEM = pl.BlockSpec(memory_space=pltpu.VMEM)
SMEM = pl.BlockSpec(memory_space=pltpu.SMEM)
PARAMS = pltpu.CompilerParams(vmem_limit_bytes=48 * 1024 * 1024)


def columns_of(index):
    return pl.ds(pl.multiple_of(index * DH, DH), DH)


def location():
    return {name: lax.axis_index(name) for name in ("yh", "z", "yl", "co")}


def bring(outside, held, arrived):
    copies = [
        pltpu.make_async_copy(source, target, arrived.at[index])
        for index, (source, target) in enumerate(zip(outside, held))
    ]
    for copy in copies:
        copy.start()
    for copy in copies:
        copy.wait()


def pack_kernel(*refs):
    outside, (own, other, split_queries), held, arrived = refs[:5], refs[5:8], refs[8:13], refs[13]
    bring(outside, held, arrived)
    cache_keys, cache_values, new_keys, new_values, queries = held
    high = location()["yh"]
    for target, head in ((own, high), (other, 1 - high)):
        columns = columns_of(head)
        for row in range(2):
            target[SLOTS * row : SLOTS * (row + 1)] = cache_keys[row, :, columns]
            target[512 + SLOTS * row : 512 + SLOTS * (row + 1)] = cache_values[row, :, columns]
        target[1024:1088] = new_keys[:, :, columns].reshape(64, DH)
        target[1088:1152] = new_values[:, :, columns].reshape(64, DH)
    for head in range(16):
        piece = queries[:, :, DH * head : DH * (head + 1)].reshape(64, DH)
        split_queries[head, 0] = piece
        split_queries[head // 8 * 8 + (head + 4) % 8, 1] = piece


def with_copies(kernel, arrays, out_shape, **options):
    return pl.pallas_call(
        kernel,
        out_shape=out_shape,
        in_specs=[pl.BlockSpec(memory_space=pl.ANY)] * len(arrays),
        out_specs=jax.tree.map(lambda _: VMEM, out_shape),
        scratch_shapes=[pltpu.VMEM(array.shape, array.dtype) for array in arrays]
        + [pltpu.SemaphoreType.DMA((len(arrays),))],
        compiler_params=pltpu.CompilerParams(vmem_limit_bytes=60 * 1024 * 1024),
        **options,
    )(*arrays)


def pack(*arrays):
    shape = jax.ShapeDtypeStruct((PART, DH), jnp.bfloat16)
    return with_copies(
        pack_kernel, arrays, (shape, shape, jax.ShapeDtypeStruct((16, 2, 64, DH), jnp.bfloat16))
    )


def score(query, key):
    return lax.dot_general(
        query, key, (((1,), (1,)), ((), ())), preferred_element_type=jnp.float32
    )


def sort_rows(flat):
    target = lax.broadcasted_iota(jnp.int32, (256, 256), 0)
    origin = lax.broadcasted_iota(jnp.int32, (256, 256), 1)
    wanted = jnp.where(target < 128, 2 * target, 2 * target - 255)
    permute = (origin == wanted).astype(jnp.float32).astype(jnp.bfloat16)
    moved = jnp.dot(permute, flat, preferred_element_type=jnp.float32).astype(jnp.bfloat16)
    return moved[:128], moved[128:]


def attend_kernel(offsets, head, skip_blocks, cache_len, queries, *refs):
    high, ring = location()["yh"], location()["z"]
    sources = [
        (high if is_own else 1 - high) * 8 + lax.rem(ring + distance, 8)
        for distance, is_own in offsets
    ]
    parts, refs = refs[: len(offsets)], refs[len(offsets) :]
    if head == 0:
        mine, own_level, sorted_queries, new_keys, new_values, scores = refs
    else:
        message, sorted_queries, new_keys, new_values, scores, statistics = refs
        statistics[...] = jnp.zeros_like(statistics)
    for group in range(4):
        flat = queries[4 * group : 4 * group + 4, head].reshape(256, DH)
        first_row, second_row = sort_rows(flat)
        sorted_queries[0, 128 * group : 128 * (group + 1)] = first_row
        sorted_queries[1, 128 * group : 128 * (group + 1)] = second_row
    for group in range(2):
        for start, sorted_rows in ((1024, new_keys), (1088, new_values)):
            flat = jnp.concatenate(
                [part[start : start + 64] for part in parts[4 * group : 4 * group + 4]], axis=0
            )
            first_row, second_row = sort_rows(flat)
            sorted_rows[0, 128 * group : 128 * (group + 1)] = first_row
            sorted_rows[1, 128 * group : 128 * (group + 1)] = second_row
    lane = lax.broadcasted_iota(jnp.int32, (1, 256), 1)
    new_token = lane % 32
    for index, source in enumerate(sources):
        new_token = new_token + jnp.where(lane // 32 == index, source * 32, 0)
    larger = (skip_blocks[1] > skip_blocks[0]).astype(jnp.int32)
    most = jnp.maximum(skip_blocks[0], skip_blocks[1])
    fewer = jnp.minimum(skip_blocks[0], skip_blocks[1])
    diagonal = lax.broadcasted_iota(jnp.int32, (128, 128), 0) == lax.broadcasted_iota(
        jnp.int32, (128, 128), 1
    )

    for index in range(3):
        row = 1 - larger if index == 1 else larger
        count = fewer if index == 1 else most
        block = 2 if index == 2 else 0
        slot = 2 if index == 2 else row
        first = jnp.where(row == 0, cache_len[0], cache_len[1]) - count * BLOCK
        key_rows = pl.ds(pl.multiple_of(row * SLOTS, SLOTS), SLOTS)
        value_rows = pl.ds(pl.multiple_of(row * SLOTS + 512, SLOTS), SLOTS)
        query = sorted_queries[row, pl.ds(block * 128, 256), :]
        peak = jnp.full((256, 128), masked_score, jnp.float32)
        spans = []
        for place_in, (part, source) in enumerate(zip(parts, sources)):
            bias = jnp.where(lane < first - source * SLOTS, 0.0, masked_score)
            found = score(query, part[key_rows]) + bias
            span = slice(SLOTS * place_in, SLOTS * (place_in + 1))
            scores[index, :, span] = found
            spans.append((span, lambda part=part: part[value_rows]))
            peak = jnp.maximum(peak, jnp.maximum(found[:, :128], found[:, 128:]))
        token = lax.broadcasted_iota(jnp.int32, (256, 1), 0) + block * 128
        found = score(query, new_keys[row])
        found = jnp.where(new_token <= token, found, masked_score)
        span = slice(SLOTS * len(parts), SLOTS * (len(parts) + 1))
        scores[index, :, span] = found
        spans.append((span, lambda: new_values[row]))
        peak = jnp.maximum(peak, jnp.maximum(found[:, :128], found[:, 128:]))
        top = jnp.broadcast_to(jnp.max(peak, axis=1, keepdims=True), (256, 128))
        total = jnp.zeros((256, 128), jnp.float32)
        mixed = jnp.zeros((256, DH), jnp.float32)
        wide = jnp.concatenate([top, top], axis=1)
        for span, values in spans:
            weight = jnp.exp2((scores[index, :, span] - wide) * exp2_scale)
            total = total + (weight[:, :128] + weight[:, 128:])
            mixed = mixed + jnp.dot(
                weight.astype(jnp.bfloat16), values(), preferred_element_type=jnp.float32
            )
        whole = jnp.broadcast_to(jnp.sum(total, axis=1, keepdims=True), (256, 128))
        result = mixed / whole
        level = top * exp2_scale + jnp.log2(whole)
        result = jnp.concatenate(
            [
                jnp.where(count > block, result[:128], 0.0),
                jnp.where(count > block + 1, result[128:], 0.0),
            ],
            axis=0,
        )
        for half in range(2):
            here = slot + 3 * half
            rows = pl.ds(here * 128, 128)
            if index < 2:
                rows = pl.ds(pl.multiple_of(here * 128, 128), 128)
            piece = result[128 * half : 128 * (half + 1)]
            piece_level = level[128 * half : 128 * (half + 1)]
            if head == 0:
                mine[rows, :] = piece
                own_level[rows, :] = piece_level
            else:
                message[rows, :] = piece.astype(jnp.bfloat16)
                flat = jnp.sum(jnp.where(diagonal, piece_level, 0.0), axis=0, keepdims=True)
                for term in range(3):
                    rounded = flat.astype(jnp.bfloat16).astype(jnp.float32)
                    statistics[pl.ds(term * 8 + here, 1), :] = rounded
                    flat = flat - rounded
    if head == 1:
        message[768:800] = statistics[...].astype(jnp.bfloat16)


def attend(counts, queries, parts, offsets, head):
    scratch = [
        pltpu.VMEM((2, 512, DH), jnp.bfloat16),
        pltpu.VMEM((2, 256, DH), jnp.bfloat16),
        pltpu.VMEM((2, 256, DH), jnp.bfloat16),
        pltpu.VMEM((3, 256, SLOTS * (len(parts) + 1)), jnp.float32),
    ]
    if head == 0:
        out_shape = (jax.ShapeDtypeStruct((768, DH), jnp.float32),) * 2
        out_specs = (VMEM,) * 2
    else:
        out_shape = jax.ShapeDtypeStruct((800, DH), jnp.bfloat16)
        out_specs = VMEM
        scratch.append(pltpu.VMEM((32, DH), jnp.float32))
    return pl.pallas_call(
        lambda *refs: attend_kernel(offsets, head, *refs),
        out_shape=out_shape,
        in_specs=[SMEM] * 2 + [VMEM] * (1 + len(parts)),
        out_specs=out_specs,
        scratch_shapes=scratch,
        compiler_params=PARAMS,
        cost_estimate=pl.CostEstimate(
            flops=5 * 10**9, bytes_accessed=6 * 2**20, transcendentals=2 * 10**6
        ),
    )(*counts, queries, *parts)


def merge_kernel(mine, own_level, message, out):
    diagonal = lax.broadcasted_iota(jnp.int32, (128, 128), 0) == lax.broadcasted_iota(
        jnp.int32, (128, 128), 1
    )
    statistics = message[768:800].astype(jnp.float32)
    for slot in range(6):
        rows = slice(128 * slot, 128 * (slot + 1))
        flat = (
            statistics[slot : slot + 1]
            + statistics[8 + slot : 9 + slot]
            + statistics[16 + slot : 17 + slot]
        )
        level = jnp.sum(jnp.where(diagonal, flat, 0.0), axis=1, keepdims=True)
        top = jnp.maximum(own_level[rows], level)
        own_weight = jnp.exp2(own_level[rows] - top)
        other_weight = jnp.exp2(level - top)
        mixed = own_weight * mine[rows] + other_weight * message[rows].astype(jnp.float32)
        out[rows] = (mixed / (own_weight + other_weight)).astype(jnp.bfloat16)


def merge(mine, own_level, message):
    return pl.pallas_call(
        merge_kernel,
        out_shape=jax.ShapeDtypeStruct((768, DH), jnp.bfloat16),
        in_specs=[VMEM] * 3,
        out_specs=VMEM,
        compiler_params=PARAMS,
    )(mine, own_level, message)


def project_kernel(first, *refs):
    ring, core = location()["z"], location()["co"]
    if first:
        attended, (weights, gathered, kept, sent) = refs[:9], refs[9:]
        for distance in range(8):
            columns = columns_of(lax.rem(ring + distance, 8))
            if distance == 4:
                gathered[:384, columns] = attended[4][...]
                gathered[384:, columns] = attended[8][...]
            else:
                gathered[:, columns] = attended[distance][...]
    else:
        gathered, weights, kept, sent = refs
    for target, owner in ((sent, 1 - core), (kept, core)):
        rows = gathered[pl.ds(pl.multiple_of(owner * 384, 128), 384), :]
        for pair in range(2):
            block = jnp.concatenate([weights[2 * pair], weights[2 * pair + 1]], axis=1)
            target[:, 256 * pair : 256 * (pair + 1)] = jnp.dot(
                rows, block, preferred_element_type=jnp.float32
            ).astype(target.dtype)


def project(arrays, weights, first):
    kept = jax.ShapeDtypeStruct((384, 512), jnp.float32)
    sent = jax.ShapeDtypeStruct((384, 512), jnp.bfloat16)
    gathered = jax.ShapeDtypeStruct((768, 1024), jnp.bfloat16)
    out_shape = (gathered, kept, sent) if first else (kept, sent)
    return pl.pallas_call(
        lambda *refs: project_kernel(first, *refs),
        out_shape=out_shape,
        in_specs=[VMEM] * (len(arrays) + 1),
        out_specs=(VMEM,) * len(out_shape),
        compiler_params=PARAMS,
        cost_estimate=pl.CostEstimate(
            flops=2 * 10**9, bytes_accessed=4 * 2**20, transcendentals=0
        ),
    )(*arrays, weights)


def add_kernel(kept, arrived, same, opposite):
    low = location()["yl"]
    total = kept[...] + arrived[...].astype(jnp.float32)
    pair = total[:256]
    single = jnp.concatenate([total[256:], jnp.zeros((128, 512), jnp.float32)], axis=0)
    same[...] = jnp.where(low == 0, pair, single).astype(same.dtype)
    opposite[...] = jnp.where(low == 0, single, pair).astype(opposite.dtype)


def add_cores(kept, arrived, dtype):
    return pl.pallas_call(
        add_kernel,
        out_shape=(
            jax.ShapeDtypeStruct((256, 512), dtype),
            jax.ShapeDtypeStruct((256, 512), jnp.bfloat16),
        ),
        in_specs=[VMEM, VMEM],
        out_specs=(VMEM,) * 2,
        compiler_params=PARAMS,
    )(kept, arrived)


def final_kernel(skip_blocks, mine, near, far, cross, out):
    low = location()["yl"]
    total = mine[...]
    for share in (near, far, cross):
        total = total + share[...].astype(jnp.float32)
    larger = skip_blocks[1] > skip_blocks[0]
    first, second = total[:128], total[128:]
    zero = jnp.zeros_like(first)
    first_row = jnp.where(low == 0, first, jnp.where(larger, zero, first))
    second_row = jnp.where(low == 0, second, jnp.where(larger, first, zero))
    out[:, 0, :] = first_row
    out[:, 1, :] = second_row


def finish(skip_blocks, *shares):
    return pl.pallas_call(
        final_kernel,
        out_shape=jax.ShapeDtypeStruct((128, 2, 512), jnp.float32),
        in_specs=[SMEM] + [VMEM] * 4,
        out_specs=VMEM,
        compiler_params=PARAMS,
    )(skip_blocks, *shares)


SWAP = [(0, 1), (1, 0)]


def ring_send(array, hops):
    return lax.ppermute(array, "z", [(index, (index + hops) % 8) for index in range(8)])


def on_device(
    queries, new_keys, new_values, cache_keys, cache_values, out_proj, skip_blocks, cache_len
):
    high = lax.axis_index("yh")
    counts = (skip_blocks, cache_len)
    own, other, split_queries = pack(cache_keys, cache_values, new_keys, new_values, queries)
    partner = lax.ppermute(other, "yh", SWAP)
    own_up, own_down = ring_send(own, 1), ring_send(own, -1)
    got_queries = lax.all_to_all(
        split_queries, ("yh", "z"), split_axis=0, concat_axis=0, tiled=True
    )
    partner_up, partner_down = ring_send(partner, 1), ring_send(partner, -1)
    own_down_two = ring_send(own_down, -1)
    tied_up, own_up = lax.optimization_barrier((partner_up, own_up))
    partner_up_two = ring_send(tied_up, 1)
    parts = [own, partner, own_up, own_down, own_down_two, partner_up, partner_down, partner_up_two]
    offsets = [
        (0, True), (0, False), (7, True), (1, True), (2, True), (7, False), (1, False), (6, False)
    ]
    out_proj, own = lax.optimization_barrier((out_proj, own))
    weights = lax.all_gather(out_proj, "row", axis=0, tiled=False)
    weights, _ = lax.optimization_barrier((weights, tied_up))
    sent_half = lax.dynamic_slice_in_dim(weights, (1 - high) * 1024, 1024, 1)
    kept_half = lax.dynamic_slice_in_dim(weights, high * 1024, 1024, 1)
    got_half = lax.ppermute(sent_half, "yh", SWAP)
    message = attend(counts, got_queries, parts, offsets, 1)
    mine, own_level = attend(counts, got_queries, parts, offsets, 0)
    attended = merge(mine, own_level, ring_send(message, 4))

    from_below, from_above = ring_send(attended, 1), ring_send(attended, -1)
    two_below, two_above = ring_send(attended, 2), ring_send(attended, -2)
    gathered = [
        attended,
        from_above,
        two_above,
        ring_send(two_above, -1),
        ring_send(two_below[:384], 2),
        ring_send(two_below, 1),
        two_below,
        from_below,
        ring_send(two_above[384:], -2),
    ]
    joined, kept, sent = project(gathered, got_half, True)
    arrived = lax.ppermute(sent, "co", SWAP)
    far, cross = add_cores(kept, arrived, jnp.bfloat16)
    joined, far = lax.optimization_barrier((joined, far))
    kept, sent = project([joined], kept_half, False)
    arrived = lax.ppermute(sent, "co", SWAP)
    mine, near = add_cores(kept, arrived, jnp.float32)
    far = lax.ppermute(far, "yh", SWAP)
    cross = lax.ppermute(cross, ("yh", "yl"), [(0, 3), (1, 2), (2, 1), (3, 0)])
    near = lax.ppermute(near, "yl", SWAP)
    return finish(skip_blocks, mine, near, far, cross)


def solution(mesh):
    split = Mesh(mesh.devices.reshape(2, 8, 2, 2, 4), ("yh", "z", "yl", "co", "row"))
    ctx, tp = ("yh", "z"), ("yl", "co")
    placed = (
        P(ctx, "row", tp),
        P(ctx, "row", tp),
        P(ctx, "row", tp),
        P("row", ctx, tp),
        P("row", ctx, tp),
        P(tp, ("yh", "z", "row")),
        P("row"),
        P("row"),
    )
    return jax.shard_map(
        on_device, mesh=split, in_specs=placed, out_specs=P(tp, "row", ctx), check_vma=False
    )
```

```python
import jax
import jax.numpy as jnp
from jax import lax
from jax.experimental import pallas as pl
from jax.experimental.pallas import tpu as pltpu
from jax.sharding import Mesh, PartitionSpec as P

DH = 128
BLOCK = 128
SLOTS = 256
PART = 1152
masked_score = -1e30
exp2_scale = DH ** -0.5 * 1.4426950408889634

VMEM = pl.BlockSpec(memory_space=pltpu.VMEM)
SMEM = pl.BlockSpec(memory_space=pltpu.SMEM)
PARAMS = pltpu.CompilerParams(vmem_limit_bytes=48 * 1024 * 1024)


def columns_of(index):
    return pl.ds(pl.multiple_of(index * DH, DH), DH)


def location():
    return {name: lax.axis_index(name) for name in ("yh", "z", "yl", "co")}


def bring(outside, held, arrived):
    copies = [
        pltpu.make_async_copy(source, target, arrived.at[index])
        for index, (source, target) in enumerate(zip(outside, held))
    ]
    for copy in copies:
        copy.start()
    for copy in copies:
        copy.wait()


def pack_kernel(*refs):
    outside, (own, other, split_queries), held, arrived = refs[:5], refs[5:8], refs[8:13], refs[13]
    bring(outside, held, arrived)
    cache_keys, cache_values, new_keys, new_values, queries = held
    high = location()["yh"]
    for target, head in ((own, high), (other, 1 - high)):
        columns = columns_of(head)
        for row in range(2):
            target[SLOTS * row : SLOTS * (row + 1)] = cache_keys[row, :, columns]
            target[512 + SLOTS * row : 512 + SLOTS * (row + 1)] = cache_values[row, :, columns]
        target[1024:1088] = new_keys[:, :, columns].reshape(64, DH)
        target[1088:1152] = new_values[:, :, columns].reshape(64, DH)
    for head in range(16):
        piece = queries[:, :, DH * head : DH * (head + 1)].reshape(64, DH)
        split_queries[head, 0] = piece
        split_queries[head // 8 * 8 + (head + 4) % 8, 1] = piece


def with_copies(kernel, arrays, out_shape, **options):
    return pl.pallas_call(
        kernel,
        out_shape=out_shape,
        in_specs=[pl.BlockSpec(memory_space=pl.ANY)] * len(arrays),
        out_specs=jax.tree.map(lambda _: VMEM, out_shape),
        scratch_shapes=[pltpu.VMEM(array.shape, array.dtype) for array in arrays]
        + [pltpu.SemaphoreType.DMA((len(arrays),))],
        compiler_params=pltpu.CompilerParams(vmem_limit_bytes=60 * 1024 * 1024),
        **options,
    )(*arrays)


def pack(*arrays):
    shape = jax.ShapeDtypeStruct((PART, DH), jnp.bfloat16)
    return with_copies(
        pack_kernel, arrays, (shape, shape, jax.ShapeDtypeStruct((16, 2, 64, DH), jnp.bfloat16))
    )


def score(query, key):
    return lax.dot_general(
        query, key, (((1,), (1,)), ((), ())), preferred_element_type=jnp.float32
    )


def sort_rows(flat):
    target = lax.broadcasted_iota(jnp.int32, (256, 256), 0)
    origin = lax.broadcasted_iota(jnp.int32, (256, 256), 1)
    wanted = jnp.where(target < 128, 2 * target, 2 * target - 255)
    permute = (origin == wanted).astype(jnp.float32).astype(jnp.bfloat16)
    moved = jnp.dot(permute, flat, preferred_element_type=jnp.float32).astype(jnp.bfloat16)
    return moved[:128], moved[128:]


def attend_kernel(offsets, head, skip_blocks, cache_len, queries, *refs):
    high, ring = location()["yh"], location()["z"]
    sources = [
        (high if is_own else 1 - high) * 8 + lax.rem(ring + distance, 8)
        for distance, is_own in offsets
    ]
    parts, refs = refs[: len(offsets)], refs[len(offsets) :]
    if head == 0:
        mine, own_level, sorted_queries, new_keys, new_values, scores = refs
    else:
        message, sorted_queries, new_keys, new_values, scores, statistics = refs
        statistics[...] = jnp.zeros_like(statistics)
    for group in range(4):
        flat = queries[4 * group : 4 * group + 4, head].reshape(256, DH)
        first_row, second_row = sort_rows(flat)
        sorted_queries[0, 128 * group : 128 * (group + 1)] = first_row
        sorted_queries[1, 128 * group : 128 * (group + 1)] = second_row
    for group in range(2):
        for start, sorted_rows in ((1024, new_keys), (1088, new_values)):
            flat = jnp.concatenate(
                [part[start : start + 64] for part in parts[4 * group : 4 * group + 4]], axis=0
            )
            first_row, second_row = sort_rows(flat)
            sorted_rows[0, 128 * group : 128 * (group + 1)] = first_row
            sorted_rows[1, 128 * group : 128 * (group + 1)] = second_row
    lane = lax.broadcasted_iota(jnp.int32, (1, 256), 1)
    new_token = lane % 32
    for index, source in enumerate(sources):
        new_token = new_token + jnp.where(lane // 32 == index, source * 32, 0)
    larger = (skip_blocks[1] > skip_blocks[0]).astype(jnp.int32)
    most = jnp.maximum(skip_blocks[0], skip_blocks[1])
    fewer = jnp.minimum(skip_blocks[0], skip_blocks[1])
    diagonal = lax.broadcasted_iota(jnp.int32, (128, 128), 0) == lax.broadcasted_iota(
        jnp.int32, (128, 128), 1
    )

    for index in range(3):
        row = 1 - larger if index == 1 else larger
        count = fewer if index == 1 else most
        block = 2 if index == 2 else 0
        slot = 2 if index == 2 else row
        first = jnp.where(row == 0, cache_len[0], cache_len[1]) - count * BLOCK
        key_rows = pl.ds(pl.multiple_of(row * SLOTS, SLOTS), SLOTS)
        value_rows = pl.ds(pl.multiple_of(row * SLOTS + 512, SLOTS), SLOTS)
        query = sorted_queries[row, pl.ds(block * 128, 256), :]
        peak = jnp.full((256, 128), masked_score, jnp.float32)
        spans = []
        for place_in, (part, source) in enumerate(zip(parts, sources)):
            bias = jnp.where(lane < first - source * SLOTS, 0.0, masked_score)
            found = score(query, part[key_rows]) + bias
            span = slice(SLOTS * place_in, SLOTS * (place_in + 1))
            scores[index, :, span] = found
            spans.append((span, lambda part=part: part[value_rows]))
            peak = jnp.maximum(peak, jnp.maximum(found[:, :128], found[:, 128:]))
        token = lax.broadcasted_iota(jnp.int32, (256, 1), 0) + block * 128
        found = score(query, new_keys[row])
        found = jnp.where(new_token <= token, found, masked_score)
        span = slice(SLOTS * len(parts), SLOTS * (len(parts) + 1))
        scores[index, :, span] = found
        spans.append((span, lambda: new_values[row]))
        peak = jnp.maximum(peak, jnp.maximum(found[:, :128], found[:, 128:]))
        top = jnp.broadcast_to(jnp.max(peak, axis=1, keepdims=True), (256, 128))
        total = jnp.zeros((256, 128), jnp.float32)
        mixed = jnp.zeros((256, DH), jnp.float32)
        wide = jnp.concatenate([top, top], axis=1)
        for span, values in spans:
            weight = jnp.exp2((scores[index, :, span] - wide) * exp2_scale)
            total = total + (weight[:, :128] + weight[:, 128:])
            mixed = mixed + jnp.dot(
                weight.astype(jnp.bfloat16), values(), preferred_element_type=jnp.float32
            )
        whole = jnp.broadcast_to(jnp.sum(total, axis=1, keepdims=True), (256, 128))
        result = mixed / whole
        level = top * exp2_scale + jnp.log2(whole)
        result = jnp.concatenate(
            [
                jnp.where(count > block, result[:128], 0.0),
                jnp.where(count > block + 1, result[128:], 0.0),
            ],
            axis=0,
        )
        for half in range(2):
            here = slot + 3 * half
            rows = pl.ds(here * 128, 128)
            if index < 2:
                rows = pl.ds(pl.multiple_of(here * 128, 128), 128)
            piece = result[128 * half : 128 * (half + 1)]
            piece_level = level[128 * half : 128 * (half + 1)]
            if head == 0:
                mine[rows, :] = piece
                own_level[rows, :] = piece_level
            else:
                message[rows, :] = piece.astype(jnp.bfloat16)
                flat = jnp.sum(jnp.where(diagonal, piece_level, 0.0), axis=0, keepdims=True)
                for term in range(3):
                    rounded = flat.astype(jnp.bfloat16).astype(jnp.float32)
                    statistics[pl.ds(term * 8 + here, 1), :] = rounded
                    flat = flat - rounded
    if head == 1:
        message[768:800] = statistics[...].astype(jnp.bfloat16)


def attend(counts, queries, parts, offsets, head):
    scratch = [
        pltpu.VMEM((2, 512, DH), jnp.bfloat16),
        pltpu.VMEM((2, 256, DH), jnp.bfloat16),
        pltpu.VMEM((2, 256, DH), jnp.bfloat16),
        pltpu.VMEM((3, 256, SLOTS * (len(parts) + 1)), jnp.float32),
    ]
    if head == 0:
        out_shape = (jax.ShapeDtypeStruct((768, DH), jnp.float32),) * 2
        out_specs = (VMEM,) * 2
    else:
        out_shape = jax.ShapeDtypeStruct((800, DH), jnp.bfloat16)
        out_specs = VMEM
        scratch.append(pltpu.VMEM((32, DH), jnp.float32))
    return pl.pallas_call(
        lambda *refs: attend_kernel(offsets, head, *refs),
        out_shape=out_shape,
        in_specs=[SMEM] * 2 + [VMEM] * (1 + len(parts)),
        out_specs=out_specs,
        scratch_shapes=scratch,
        compiler_params=PARAMS,
        cost_estimate=pl.CostEstimate(
            flops=5 * 10**9, bytes_accessed=6 * 2**20, transcendentals=2 * 10**6
        ),
    )(*counts, queries, *parts)


def merge_kernel(mine, own_level, message, out):
    diagonal = lax.broadcasted_iota(jnp.int32, (128, 128), 0) == lax.broadcasted_iota(
        jnp.int32, (128, 128), 1
    )
    statistics = message[768:800].astype(jnp.float32)
    for slot in range(6):
        rows = slice(128 * slot, 128 * (slot + 1))
        flat = (
            statistics[slot : slot + 1]
            + statistics[8 + slot : 9 + slot]
            + statistics[16 + slot : 17 + slot]
        )
        level = jnp.sum(jnp.where(diagonal, flat, 0.0), axis=1, keepdims=True)
        top = jnp.maximum(own_level[rows], level)
        own_weight = jnp.exp2(own_level[rows] - top)
        other_weight = jnp.exp2(level - top)
        mixed = own_weight * mine[rows] + other_weight * message[rows].astype(jnp.float32)
        out[rows] = (mixed / (own_weight + other_weight)).astype(jnp.bfloat16)


def merge(mine, own_level, message):
    return pl.pallas_call(
        merge_kernel,
        out_shape=jax.ShapeDtypeStruct((768, DH), jnp.bfloat16),
        in_specs=[VMEM] * 3,
        out_specs=VMEM,
        compiler_params=PARAMS,
    )(mine, own_level, message)


def project_kernel(first, *refs):
    ring, core = location()["z"], location()["co"]
    if first:
        attended, (weights, gathered, kept, sent) = refs[:9], refs[9:]
        for distance in range(8):
            columns = columns_of(lax.rem(ring + distance, 8))
            if distance == 4:
                gathered[:384, columns] = attended[4][...]
                gathered[384:, columns] = attended[8][...]
            else:
                gathered[:, columns] = attended[distance][...]
    else:
        gathered, weights, kept, sent = refs
    for target, owner in ((sent, 1 - core), (kept, core)):
        rows = gathered[pl.ds(pl.multiple_of(owner * 384, 128), 384), :]
        for pair in range(2):
            block = jnp.concatenate([weights[2 * pair], weights[2 * pair + 1]], axis=1)
            target[:, 256 * pair : 256 * (pair + 1)] = jnp.dot(
                rows, block, preferred_element_type=jnp.float32
            ).astype(target.dtype)


def project(arrays, weights, first):
    kept = jax.ShapeDtypeStruct((384, 512), jnp.float32)
    sent = jax.ShapeDtypeStruct((384, 512), jnp.bfloat16)
    gathered = jax.ShapeDtypeStruct((768, 1024), jnp.bfloat16)
    out_shape = (gathered, kept, sent) if first else (kept, sent)
    return pl.pallas_call(
        lambda *refs: project_kernel(first, *refs),
        out_shape=out_shape,
        in_specs=[VMEM] * (len(arrays) + 1),
        out_specs=(VMEM,) * len(out_shape),
        compiler_params=PARAMS,
        cost_estimate=pl.CostEstimate(
            flops=2 * 10**9, bytes_accessed=4 * 2**20, transcendentals=0
        ),
    )(*arrays, weights)


def add_kernel(kept, arrived, same, opposite):
    low = location()["yl"]
    total = kept[...] + arrived[...].astype(jnp.float32)
    pair = total[:256]
    single = jnp.concatenate([total[256:], jnp.zeros((128, 512), jnp.float32)], axis=0)
    same[...] = jnp.where(low == 0, pair, single).astype(same.dtype)
    opposite[...] = jnp.where(low == 0, single, pair).astype(opposite.dtype)


def add_cores(kept, arrived, dtype):
    return pl.pallas_call(
        add_kernel,
        out_shape=(
            jax.ShapeDtypeStruct((256, 512), dtype),
            jax.ShapeDtypeStruct((256, 512), jnp.bfloat16),
        ),
        in_specs=[VMEM, VMEM],
        out_specs=(VMEM,) * 2,
        compiler_params=PARAMS,
    )(kept, arrived)


def final_kernel(skip_blocks, mine, near, far, cross, out):
    low = location()["yl"]
    total = mine[...]
    for share in (near, far, cross):
        total = total + share[...].astype(jnp.float32)
    larger = skip_blocks[1] > skip_blocks[0]
    first, second = total[:128], total[128:]
    zero = jnp.zeros_like(first)
    first_row = jnp.where(low == 0, first, jnp.where(larger, zero, first))
    second_row = jnp.where(low == 0, second, jnp.where(larger, first, zero))
    out[:, 0, :] = first_row
    out[:, 1, :] = second_row


def finish(skip_blocks, *shares):
    return pl.pallas_call(
        final_kernel,
        out_shape=jax.ShapeDtypeStruct((128, 2, 512), jnp.float32),
        in_specs=[SMEM] + [VMEM] * 4,
        out_specs=VMEM,
        compiler_params=PARAMS,
    )(skip_blocks, *shares)


SWAP = [(0, 1), (1, 0)]


def ring_send(array, hops):
    return lax.ppermute(array, "z", [(index, (index + hops) % 8) for index in range(8)])


def on_device(
    queries, new_keys, new_values, cache_keys, cache_values, out_proj, skip_blocks, cache_len
):
    high = lax.axis_index("yh")
    counts = (skip_blocks, cache_len)
    own, other, split_queries = pack(cache_keys, cache_values, new_keys, new_values, queries)
    partner = lax.ppermute(other, "yh", SWAP)
    own_up, own_down = ring_send(own, 1), ring_send(own, -1)
    got_queries = lax.all_to_all(
        split_queries, ("yh", "z"), split_axis=0, concat_axis=0, tiled=True
    )
    partner_up, partner_down = ring_send(partner, 1), ring_send(partner, -1)
    own_down, own_up = lax.optimization_barrier((own_down, own_up))
    own_down_two = ring_send(own_down, -1)
    partner_up_two = ring_send(partner_up, 1)
    parts = [own, partner, own_up, own_down, own_down_two, partner_up, partner_down, partner_up_two]
    offsets = [
        (0, True), (0, False), (7, True), (1, True), (2, True), (7, False), (1, False), (6, False)
    ]
    out_proj, own = lax.optimization_barrier((out_proj, own))
    weights = lax.all_gather(out_proj, "row", axis=0, tiled=False)
    weights, _ = lax.optimization_barrier((weights, partner_up))
    sent_half = lax.dynamic_slice_in_dim(weights, (1 - high) * 1024, 1024, 1)
    kept_half = lax.dynamic_slice_in_dim(weights, high * 1024, 1024, 1)
    got_half = lax.ppermute(sent_half, "yh", SWAP)
    message = attend(counts, got_queries, parts, offsets, 1)
    mine, own_level = attend(counts, got_queries, parts, offsets, 0)
    attended = merge(mine, own_level, ring_send(message, 4))

    from_below, from_above = ring_send(attended, 1), ring_send(attended, -1)
    two_below, two_above = ring_send(attended, 2), ring_send(attended, -2)
    gathered = [
        attended,
        from_above,
        two_above,
        ring_send(two_above, -1),
        ring_send(two_below[:384], 2),
        ring_send(two_below, 1),
        two_below,
        from_below,
        ring_send(two_above[384:], -2),
    ]
    joined, kept, sent = project(gathered, got_half, True)
    arrived = lax.ppermute(sent, "co", SWAP)
    far, cross = add_cores(kept, arrived, jnp.bfloat16)
    joined, far = lax.optimization_barrier((joined, far))
    kept, sent = project([joined], kept_half, False)
    arrived = lax.ppermute(sent, "co", SWAP)
    mine, near = add_cores(kept, arrived, jnp.float32)
    far = lax.ppermute(far, "yh", SWAP)
    cross = lax.ppermute(cross, ("yh", "yl"), [(0, 3), (1, 2), (2, 1), (3, 0)])
    near = lax.ppermute(near, "yl", SWAP)
    return finish(skip_blocks, mine, near, far, cross)


def solution(mesh):
    split = Mesh(mesh.devices.reshape(2, 8, 2, 2, 4), ("yh", "z", "yl", "co", "row"))
    ctx, tp = ("yh", "z"), ("yl", "co")
    placed = (
        P(ctx, "row", tp),
        P(ctx, "row", tp),
        P(ctx, "row", tp),
        P("row", ctx, tp),
        P("row", ctx, tp),
        P(tp, ("yh", "z", "row")),
        P("row"),
        P("row"),
    )
    return jax.shard_map(
        on_device, mesh=split, in_specs=placed, out_specs=P(tp, "row", ctx), check_vma=False
    )
```

```python
import jax
import jax.numpy as jnp
from jax import lax
from jax.experimental import pallas as pl
from jax.experimental.pallas import tpu as pltpu
from jax.sharding import Mesh, PartitionSpec as P

DH = 128
BLOCK = 128
SLOTS = 256
PART = 1152
masked_score = -1e30
exp2_scale = DH ** -0.5 * 1.4426950408889634

VMEM = pl.BlockSpec(memory_space=pltpu.VMEM)
SMEM = pl.BlockSpec(memory_space=pltpu.SMEM)
PARAMS = pltpu.CompilerParams(vmem_limit_bytes=48 * 1024 * 1024)


def columns_of(index):
    return pl.ds(pl.multiple_of(index * DH, DH), DH)


def location():
    return {name: lax.axis_index(name) for name in ("yh", "z", "yl", "co")}


def bring(outside, held, arrived):
    copies = [
        pltpu.make_async_copy(source, target, arrived.at[index])
        for index, (source, target) in enumerate(zip(outside, held))
    ]
    for copy in copies:
        copy.start()
    for copy in copies:
        copy.wait()


def pack_kernel(*refs):
    outside, (own, other, split_queries), held, arrived = refs[:5], refs[5:8], refs[8:13], refs[13]
    bring(outside, held, arrived)
    cache_keys, cache_values, new_keys, new_values, queries = held
    high = location()["yh"]
    for target, head in ((own, high), (other, 1 - high)):
        columns = columns_of(head)
        for row in range(2):
            target[SLOTS * row : SLOTS * (row + 1)] = cache_keys[row, :, columns]
            target[512 + SLOTS * row : 512 + SLOTS * (row + 1)] = cache_values[row, :, columns]
        target[1024:1088] = new_keys[:, :, columns].reshape(64, DH)
        target[1088:1152] = new_values[:, :, columns].reshape(64, DH)
    for head in range(16):
        piece = queries[:, :, DH * head : DH * (head + 1)].reshape(64, DH)
        split_queries[head, 0] = piece
        split_queries[head // 8 * 8 + (head + 4) % 8, 1] = piece


def with_copies(kernel, arrays, out_shape, **options):
    return pl.pallas_call(
        kernel,
        out_shape=out_shape,
        in_specs=[pl.BlockSpec(memory_space=pl.ANY)] * len(arrays),
        out_specs=jax.tree.map(lambda _: VMEM, out_shape),
        scratch_shapes=[pltpu.VMEM(array.shape, array.dtype) for array in arrays]
        + [pltpu.SemaphoreType.DMA((len(arrays),))],
        compiler_params=pltpu.CompilerParams(vmem_limit_bytes=60 * 1024 * 1024),
        **options,
    )(*arrays)


def pack(*arrays):
    shape = jax.ShapeDtypeStruct((PART, DH), jnp.bfloat16)
    return with_copies(
        pack_kernel, arrays, (shape, shape, jax.ShapeDtypeStruct((16, 2, 64, DH), jnp.bfloat16))
    )


def score(query, key):
    return lax.dot_general(
        query, key, (((1,), (1,)), ((), ())), preferred_element_type=jnp.float32
    )


def sort_rows(flat):
    target = lax.broadcasted_iota(jnp.int32, (256, 256), 0)
    origin = lax.broadcasted_iota(jnp.int32, (256, 256), 1)
    wanted = jnp.where(target < 128, 2 * target, 2 * target - 255)
    permute = (origin == wanted).astype(jnp.float32).astype(jnp.bfloat16)
    moved = jnp.dot(permute, flat, preferred_element_type=jnp.float32).astype(jnp.bfloat16)
    return moved[:128], moved[128:]


def attend_kernel(offsets, head, skip_blocks, cache_len, queries, *refs):
    high, ring = location()["yh"], location()["z"]
    sources = [
        (high if is_own else 1 - high) * 8 + lax.rem(ring + distance, 8)
        for distance, is_own in offsets
    ]
    parts, refs = refs[: len(offsets)], refs[len(offsets) :]
    if head == 0:
        mine, own_level, sorted_queries, new_keys, new_values, scores = refs
    else:
        message, sorted_queries, new_keys, new_values, scores, statistics = refs
        statistics[...] = jnp.zeros_like(statistics)
    for group in range(4):
        flat = queries[4 * group : 4 * group + 4, head].reshape(256, DH)
        first_row, second_row = sort_rows(flat)
        sorted_queries[0, 128 * group : 128 * (group + 1)] = first_row
        sorted_queries[1, 128 * group : 128 * (group + 1)] = second_row
    for group in range(2):
        for start, sorted_rows in ((1024, new_keys), (1088, new_values)):
            flat = jnp.concatenate(
                [part[start : start + 64] for part in parts[4 * group : 4 * group + 4]], axis=0
            )
            first_row, second_row = sort_rows(flat)
            sorted_rows[0, 128 * group : 128 * (group + 1)] = first_row
            sorted_rows[1, 128 * group : 128 * (group + 1)] = second_row
    lane = lax.broadcasted_iota(jnp.int32, (1, 256), 1)
    new_token = lane % 32
    for index, source in enumerate(sources):
        new_token = new_token + jnp.where(lane // 32 == index, source * 32, 0)
    larger = (skip_blocks[1] > skip_blocks[0]).astype(jnp.int32)
    most = jnp.maximum(skip_blocks[0], skip_blocks[1])
    fewer = jnp.minimum(skip_blocks[0], skip_blocks[1])
    diagonal = lax.broadcasted_iota(jnp.int32, (128, 128), 0) == lax.broadcasted_iota(
        jnp.int32, (128, 128), 1
    )

    for index in range(3):
        row = 1 - larger if index == 1 else larger
        count = fewer if index == 1 else most
        block = 2 if index == 2 else 0
        slot = 2 if index == 2 else row
        first = jnp.where(row == 0, cache_len[0], cache_len[1]) - count * BLOCK
        key_rows = pl.ds(pl.multiple_of(row * SLOTS, SLOTS), SLOTS)
        value_rows = pl.ds(pl.multiple_of(row * SLOTS + 512, SLOTS), SLOTS)
        query = sorted_queries[row, pl.ds(block * 128, 256), :]
        peak = jnp.full((256, 128), masked_score, jnp.float32)
        spans = []
        for place_in, (part, source) in enumerate(zip(parts, sources)):
            bias = jnp.where(lane < first - source * SLOTS, 0.0, masked_score)
            found = score(query, part[key_rows]) + bias
            span = slice(SLOTS * place_in, SLOTS * (place_in + 1))
            scores[index, :, span] = found
            spans.append((span, lambda part=part: part[value_rows]))
            peak = jnp.maximum(peak, jnp.maximum(found[:, :128], found[:, 128:]))
        token = lax.broadcasted_iota(jnp.int32, (256, 1), 0) + block * 128
        found = score(query, new_keys[row])
        found = jnp.where(new_token <= token, found, masked_score)
        span = slice(SLOTS * len(parts), SLOTS * (len(parts) + 1))
        scores[index, :, span] = found
        spans.append((span, lambda: new_values[row]))
        peak = jnp.maximum(peak, jnp.maximum(found[:, :128], found[:, 128:]))
        top = jnp.broadcast_to(jnp.max(peak, axis=1, keepdims=True), (256, 128))
        total = jnp.zeros((256, 128), jnp.float32)
        mixed = jnp.zeros((256, DH), jnp.float32)
        wide = jnp.concatenate([top, top], axis=1)
        for span, values in spans:
            weight = jnp.exp2((scores[index, :, span] - wide) * exp2_scale)
            total = total + (weight[:, :128] + weight[:, 128:])
            mixed = mixed + jnp.dot(
                weight.astype(jnp.bfloat16), values(), preferred_element_type=jnp.float32
            )
        whole = jnp.broadcast_to(jnp.sum(total, axis=1, keepdims=True), (256, 128))
        result = mixed / whole
        level = top * exp2_scale + jnp.log2(whole)
        result = jnp.concatenate(
            [
                jnp.where(count > block, result[:128], 0.0),
                jnp.where(count > block + 1, result[128:], 0.0),
            ],
            axis=0,
        )
        for half in range(2):
            here = slot + 3 * half
            rows = pl.ds(here * 128, 128)
            if index < 2:
                rows = pl.ds(pl.multiple_of(here * 128, 128), 128)
            piece = result[128 * half : 128 * (half + 1)]
            piece_level = level[128 * half : 128 * (half + 1)]
            if head == 0:
                mine[rows, :] = piece
                own_level[rows, :] = piece_level
            else:
                message[rows, :] = piece.astype(jnp.bfloat16)
                flat = jnp.sum(jnp.where(diagonal, piece_level, 0.0), axis=0, keepdims=True)
                for term in range(3):
                    rounded = flat.astype(jnp.bfloat16).astype(jnp.float32)
                    statistics[pl.ds(term * 8 + here, 1), :] = rounded
                    flat = flat - rounded
    if head == 1:
        message[768:800] = statistics[...].astype(jnp.bfloat16)


def attend(counts, queries, parts, offsets, head):
    scratch = [
        pltpu.VMEM((2, 512, DH), jnp.bfloat16),
        pltpu.VMEM((2, 256, DH), jnp.bfloat16),
        pltpu.VMEM((2, 256, DH), jnp.bfloat16),
        pltpu.VMEM((3, 256, SLOTS * (len(parts) + 1)), jnp.float32),
    ]
    if head == 0:
        out_shape = (jax.ShapeDtypeStruct((768, DH), jnp.float32),) * 2
        out_specs = (VMEM,) * 2
    else:
        out_shape = jax.ShapeDtypeStruct((800, DH), jnp.bfloat16)
        out_specs = VMEM
        scratch.append(pltpu.VMEM((32, DH), jnp.float32))
    return pl.pallas_call(
        lambda *refs: attend_kernel(offsets, head, *refs),
        out_shape=out_shape,
        in_specs=[SMEM] * 2 + [VMEM] * (1 + len(parts)),
        out_specs=out_specs,
        scratch_shapes=scratch,
        compiler_params=pltpu.CompilerParams(vmem_limit_bytes=56 * 1024 * 1024),
        cost_estimate=pl.CostEstimate(
            flops=5 * 10**9, bytes_accessed=6 * 2**20, transcendentals=2 * 10**6
        ),
    )(*counts, queries, *parts)


def merge_kernel(mine, own_level, message, out):
    diagonal = lax.broadcasted_iota(jnp.int32, (128, 128), 0) == lax.broadcasted_iota(
        jnp.int32, (128, 128), 1
    )
    statistics = message[768:800].astype(jnp.float32)
    for slot in range(6):
        rows = slice(128 * slot, 128 * (slot + 1))
        flat = (
            statistics[slot : slot + 1]
            + statistics[8 + slot : 9 + slot]
            + statistics[16 + slot : 17 + slot]
        )
        level = jnp.sum(jnp.where(diagonal, flat, 0.0), axis=1, keepdims=True)
        top = jnp.maximum(own_level[rows], level)
        own_weight = jnp.exp2(own_level[rows] - top)
        other_weight = jnp.exp2(level - top)
        mixed = own_weight * mine[rows] + other_weight * message[rows].astype(jnp.float32)
        out[rows] = (mixed / (own_weight + other_weight)).astype(jnp.bfloat16)


def merge(mine, own_level, message):
    return pl.pallas_call(
        merge_kernel,
        out_shape=jax.ShapeDtypeStruct((768, DH), jnp.bfloat16),
        in_specs=[VMEM] * 3,
        out_specs=VMEM,
        compiler_params=PARAMS,
    )(mine, own_level, message)


def project_kernel(first, *refs):
    ring, core = location()["z"], location()["co"]
    if first:
        attended, (weights, gathered, kept, sent) = refs[:9], refs[9:]
        for distance in range(8):
            columns = columns_of(lax.rem(ring + distance, 8))
            if distance == 4:
                gathered[:384, columns] = attended[4][...]
                gathered[384:, columns] = attended[8][...]
            else:
                gathered[:, columns] = attended[distance][...]
    else:
        gathered, weights, kept, sent = refs
    for target, owner in ((sent, 1 - core), (kept, core)):
        rows = gathered[pl.ds(pl.multiple_of(owner * 384, 128), 384), :]
        for pair in range(2):
            block = jnp.concatenate([weights[2 * pair], weights[2 * pair + 1]], axis=1)
            target[:, 256 * pair : 256 * (pair + 1)] = jnp.dot(
                rows, block, preferred_element_type=jnp.float32
            ).astype(target.dtype)


def project(arrays, weights, first):
    kept = jax.ShapeDtypeStruct((384, 512), jnp.float32)
    sent = jax.ShapeDtypeStruct((384, 512), jnp.bfloat16)
    gathered = jax.ShapeDtypeStruct((768, 1024), jnp.bfloat16)
    out_shape = (gathered, kept, sent) if first else (kept, sent)
    return pl.pallas_call(
        lambda *refs: project_kernel(first, *refs),
        out_shape=out_shape,
        in_specs=[VMEM] * (len(arrays) + 1),
        out_specs=(VMEM,) * len(out_shape),
        compiler_params=PARAMS,
        cost_estimate=pl.CostEstimate(
            flops=2 * 10**9, bytes_accessed=4 * 2**20, transcendentals=0
        ),
    )(*arrays, weights)


def add_kernel(kept, arrived, same, opposite):
    low = location()["yl"]
    total = kept[...] + arrived[...].astype(jnp.float32)
    pair = total[:256]
    single = jnp.concatenate([total[256:], jnp.zeros((128, 512), jnp.float32)], axis=0)
    same[...] = jnp.where(low == 0, pair, single).astype(same.dtype)
    opposite[...] = jnp.where(low == 0, single, pair).astype(opposite.dtype)


def add_cores(kept, arrived, dtype):
    return pl.pallas_call(
        add_kernel,
        out_shape=(
            jax.ShapeDtypeStruct((256, 512), dtype),
            jax.ShapeDtypeStruct((256, 512), jnp.bfloat16),
        ),
        in_specs=[VMEM, VMEM],
        out_specs=(VMEM,) * 2,
        compiler_params=PARAMS,
    )(kept, arrived)


def final_kernel(skip_blocks, mine, near, far, cross, out):
    low = location()["yl"]
    total = mine[...]
    for share in (near, far, cross):
        total = total + share[...].astype(jnp.float32)
    larger = skip_blocks[1] > skip_blocks[0]
    first, second = total[:128], total[128:]
    zero = jnp.zeros_like(first)
    first_row = jnp.where(low == 0, first, jnp.where(larger, zero, first))
    second_row = jnp.where(low == 0, second, jnp.where(larger, first, zero))
    out[:, 0, :] = first_row
    out[:, 1, :] = second_row


def finish(skip_blocks, *shares):
    return pl.pallas_call(
        final_kernel,
        out_shape=jax.ShapeDtypeStruct((128, 2, 512), jnp.float32),
        in_specs=[SMEM] + [VMEM] * 4,
        out_specs=VMEM,
        compiler_params=PARAMS,
    )(skip_blocks, *shares)


SWAP = [(0, 1), (1, 0)]


def ring_send(array, hops):
    return lax.ppermute(array, "z", [(index, (index + hops) % 8) for index in range(8)])


def on_device(
    queries, new_keys, new_values, cache_keys, cache_values, out_proj, skip_blocks, cache_len
):
    high = lax.axis_index("yh")
    counts = (skip_blocks, cache_len)
    own, other, split_queries = pack(cache_keys, cache_values, new_keys, new_values, queries)
    partner = lax.ppermute(other, "yh", SWAP)
    own_up, own_down = ring_send(own, 1), ring_send(own, -1)
    got_queries = lax.all_to_all(
        split_queries, ("yh", "z"), split_axis=0, concat_axis=0, tiled=True
    )
    partner_up, partner_down = ring_send(partner, 1), ring_send(partner, -1)
    own_down_two = ring_send(own_down, -1)
    tied_up, own_up = lax.optimization_barrier((partner_up, own_up))
    partner_up_two = ring_send(tied_up, 1)
    parts = [own, partner, own_up, own_down, own_down_two, partner_up, partner_down, partner_up_two]
    offsets = [
        (0, True), (0, False), (7, True), (1, True), (2, True), (7, False), (1, False), (6, False)
    ]
    out_proj, own = lax.optimization_barrier((out_proj, own))
    weights = lax.all_gather(out_proj, "row", axis=0, tiled=False)
    weights, _ = lax.optimization_barrier((weights, tied_up))
    sent_half = lax.dynamic_slice_in_dim(weights, (1 - high) * 1024, 1024, 1)
    kept_half = lax.dynamic_slice_in_dim(weights, high * 1024, 1024, 1)
    got_half = lax.ppermute(sent_half, "yh", SWAP)
    message = attend(counts, got_queries, parts, offsets, 1)
    mine, own_level = attend(counts, got_queries, parts, offsets, 0)
    attended = merge(mine, own_level, ring_send(message, 4))

    from_below, from_above = ring_send(attended, 1), ring_send(attended, -1)
    two_below, two_above = ring_send(attended, 2), ring_send(attended, -2)
    gathered = [
        attended,
        from_above,
        two_above,
        ring_send(two_above, -1),
        ring_send(two_below[:384], 2),
        ring_send(two_below, 1),
        two_below,
        from_below,
        ring_send(two_above[384:], -2),
    ]
    joined, kept, sent = project(gathered, got_half, True)
    arrived = lax.ppermute(sent, "co", SWAP)
    far, cross = add_cores(kept, arrived, jnp.bfloat16)
    joined, far = lax.optimization_barrier((joined, far))
    kept, sent = project([joined], kept_half, False)
    arrived = lax.ppermute(sent, "co", SWAP)
    mine, near = add_cores(kept, arrived, jnp.float32)
    far = lax.ppermute(far, "yh", SWAP)
    cross = lax.ppermute(cross, ("yh", "yl"), [(0, 3), (1, 2), (2, 1), (3, 0)])
    near = lax.ppermute(near, "yl", SWAP)
    return finish(skip_blocks, mine, near, far, cross)


def solution(mesh):
    split = Mesh(mesh.devices.reshape(2, 8, 2, 2, 4), ("yh", "z", "yl", "co", "row"))
    ctx, tp = ("yh", "z"), ("yl", "co")
    placed = (
        P(ctx, "row", tp),
        P(ctx, "row", tp),
        P(ctx, "row", tp),
        P("row", ctx, tp),
        P("row", ctx, tp),
        P(tp, ("yh", "z", "row")),
        P("row"),
        P("row"),
    )
    return jax.shard_map(
        on_device, mesh=split, in_specs=placed, out_specs=P(tp, "row", ctx), check_vma=False
    )
```
